32 devices in a mesh: section: 4 (over y, core), dp: 8 (over z, x).
Axes of the slice: x: 2, y: 2, z: 4, core: 2. Of those that a mesh axis runs over, the one named last changes fastest.
Arguments:
- token_states: bfloat16 [4, 128, 8192], P(None, 'dp'), may hold values from -10 to 10
- norm_gains: float32 [4, 8192], P('section'), may hold values from 1 to 4
- prompt_kv: bfloat16 [4, 1024, 2048], P('section'), may hold values from -11 to 11
- history_kv: bfloat16 [4, 128, 28, 2048], P('section', 'dp'), may hold values from -6 to 6
- new_kv: bfloat16 [4, 4, 128, 2048], P('section', None, 'dp'), may hold values from -6 to 6
- ancestors: int32 [128], replicated, may hold values from 0 to 127, as said below
Outputs:
- attention_out: bfloat16 [4, 4, 128, 8192], P('section', None, 'dp')
- forked_kv: bfloat16 [4, 128, 32, 2048], P('section', 'dp')
The draws below stay inside these ranges and needn't reach their ends.
Inputs may be any that keep to these rules, and one draw needn't show every extreme that they name: Of the 16 ancestors of particles p * 16 .. p * 16 + 15, at most one distinct value lies in any block q * 16 .. q * 16 + 15; ancestors may repeat.
All inputs are finite; a program needn't handle non-finite values.
Results may differ from the reference program's by a relative error of at most 0.0086.
Values may be sent and summed in bfloat16 or wider, within the bound.
A program may use at most 128 MiB of HBM per device.

```python
import math
import jax
import jax.numpy as jnp
from jax import lax

D = 8192
HEADS = 64
KV_HEADS = 8
HEAD_DIM = 128
KVW = 2048
STEPS = 4
PROMPT = 1024
HIST = 28
PART_DEV = 16
LAYERS = 4
PARTICLES = 128


def draw_ancestors(key, part):
    shard_count = PARTICLES // PART_DEV
    chosen = min(PART_DEV // 2, shard_count)

    def one_shard(index):
        inner = jax.random.fold_in(jax.random.fold_in(key, 7919), index)
        shard_key, pick_key, extra_key, order_key = jax.random.split(inner, 4)
        sources = jax.random.permutation(shard_key, shard_count)[:chosen]
        within = jax.random.randint(pick_key, (chosen,), 0, PART_DEV)
        distinct = sources * PART_DEV + within
        repeats = jax.random.randint(extra_key, (PART_DEV - chosen,), 0, chosen)
        slots = jnp.concatenate([distinct, distinct[repeats]])
        order = jax.random.permutation(order_key, PART_DEV)
        return slots[order]
    table = jax.vmap(one_shard)(jnp.arange(shard_count))
    return table.reshape(PARTICLES).astype(jnp.int32)


def draw_token_states(key, part):
    jitter_key = jax.random.fold_in(jax.random.fold_in(key, 11), 0)
    array_shape = (STEPS, PARTICLES, D)
    return jnp.clip(jax.random.normal(jitter_key, array_shape, jnp.float32), -6.0, 6.0).astype(jnp.bfloat16)


def draw_norm_gains(key, part):
    spread = jax.random.uniform(jax.random.fold_in(key, 23), (LAYERS, D), jnp.float32, 0.0, math.log(4.0))
    return jnp.exp(spread)


def draw_prompt_kv(key, part):
    base_key = jax.random.fold_in(jax.random.fold_in(key, 31), 0)
    array_shape = (LAYERS, PROMPT, KVW)
    return jnp.clip(jax.random.normal(base_key, array_shape, jnp.float32), -6.0, 6.0).astype(jnp.bfloat16)


def steps_of(stream_key, shape, cuts, least, largest):
    gain = 1.0
    for axis_at, blocks in cuts:
        steps = jax.random.uniform(jax.random.fold_in(jax.random.fold_in(stream_key, 6), axis_at), (blocks,), jnp.float32, least / len(cuts), largest / len(cuts))
        gain = gain * jnp.repeat(jnp.exp(steps), shape[axis_at] // blocks).reshape((-1,) + (1,) * (len(shape) - 1 - axis_at))
    return gain


def noise(stream_key, shape, scale, bound, cuts=(), held_as=jnp.bfloat16):
    level = steps_of(stream_key, shape, cuts, -0.22, 0.18) if cuts else 1.0
    drawn = jax.random.normal(stream_key, shape, jnp.float32) * scale * level
    return jnp.minimum(jnp.maximum(drawn, -bound), bound).astype(held_as)


def setup_inputs(seed: int = 0) -> dict:
    key_of = jax.random.split(jax.random.key(seed), 7)
    token_states = draw_token_states(jax.random.fold_in(key_of[6], 71), 0)
    norm_gains = draw_norm_gains(jax.random.fold_in(key_of[6], 71), 0)
    prompt_kv = draw_prompt_kv(jax.random.fold_in(key_of[6], 71), 0)
    history_kv = noise(key_of[3], (LAYERS, PARTICLES, HIST, KVW), 1.0, 6.0, ((0, 4), (1, 8)))
    new_kv = noise(key_of[4], (LAYERS, STEPS, PARTICLES, KVW), 1.0, 6.0, ((0, 4), (2, 8)))
    ancestors = draw_ancestors(jax.random.fold_in(key_of[6], 71), 0)
    return dict(token_states=token_states, norm_gains=norm_gains, prompt_kv=prompt_kv, history_kv=history_kv, new_kv=new_kv, ancestors=ancestors)


NEG_FILL = -1e+30

def normalize(values):
    return values * lax.rsqrt(lax.optimization_barrier(jnp.mean(values * values, axis=-1, keepdims=True)) + 1e-05)

def attend(hidden, gains_row, prompt, history, recent, step_now):
    rows = hidden.shape[0]
    half = KV_HEADS * HEAD_DIM
    share = HEADS // KV_HEADS
    rounded = (normalize(hidden) * gains_row).astype(jnp.bfloat16)
    queries = lax.optimization_barrier(rounded).astype(jnp.float32).reshape(rows, KV_HEADS, share, HEAD_DIM)
    prompt_keys = prompt[:, :half].astype(jnp.float32).reshape(-1, KV_HEADS, HEAD_DIM)
    prompt_vals = prompt[:, half:].astype(jnp.float32).reshape(-1, KV_HEADS, HEAD_DIM)
    past_keys = history[..., :half].astype(jnp.float32).reshape(rows, -1, KV_HEADS, HEAD_DIM)
    past_vals = history[..., half:].astype(jnp.float32).reshape(rows, -1, KV_HEADS, HEAD_DIM)
    recent_keys = recent[..., :half].astype(jnp.float32).reshape(-1, rows, KV_HEADS, HEAD_DIM)
    recent_vals = recent[..., half:].astype(jnp.float32).reshape(-1, rows, KV_HEADS, HEAD_DIM)
    score_scale = HEAD_DIM ** (-0.5)
    prompt_scores = jnp.einsum('pkgd,nkd->pkgn', queries, prompt_keys) * score_scale
    past_scores = jnp.einsum('pkgd,pnkd->pkgn', queries, past_keys) * score_scale
    recent_scores = jnp.einsum('pkgd,npkd->pkgn', queries, recent_keys) * score_scale
    present = jnp.arange(recent.shape[0]) <= step_now
    recent_scores = jnp.where(present, recent_scores, NEG_FILL)
    highest = jnp.maximum(lax.optimization_barrier(jnp.max(prompt_scores, -1, keepdims=True)), lax.optimization_barrier(jnp.max(past_scores, -1, keepdims=True)))
    highest = jnp.maximum(highest, lax.optimization_barrier(jnp.max(recent_scores, -1, keepdims=True)))
    prompt_exp = jnp.exp(prompt_scores - highest)
    past_exp = jnp.exp(past_scores - highest)
    recent_exp = jnp.exp(recent_scores - highest)
    denominator = lax.optimization_barrier(jnp.sum(prompt_exp, -1, keepdims=True)) + lax.optimization_barrier(jnp.sum(past_exp, -1, keepdims=True)) + lax.optimization_barrier(jnp.sum(recent_exp, -1, keepdims=True))

    def weigh(portion):
        return lax.optimization_barrier((portion / denominator).astype(jnp.bfloat16)).astype(jnp.float32)
    mixed = jnp.einsum('pkgn,nkd->pkgd', weigh(prompt_exp), prompt_vals)
    mixed = mixed + jnp.einsum('pkgn,pnkd->pkgd', weigh(past_exp), past_vals)
    mixed = mixed + jnp.einsum('pkgn,npkd->pkgd', weigh(recent_exp), recent_vals)
    return mixed.reshape(rows, HEADS * HEAD_DIM)

def reference(token_states, norm_gains, prompt_kv, history_kv, new_kv, ancestors):
    layer_count = norm_gains.shape[0]
    results = [[None] * STEPS for layer in range(layer_count)]
    previous = None
    for step in range(STEPS):
        residual = token_states[step].astype(jnp.float32)
        if step > 0:
            residual = residual + normalize(previous)
        for layer in range(layer_count):
            mixed = attend(residual, norm_gains[layer], prompt_kv[layer], history_kv[layer], new_kv[layer], step)
            results[layer][step] = mixed.astype(jnp.bfloat16)
            residual = residual + mixed
        previous = residual
    attention_out = jnp.stack([jnp.stack(results[layer], 0) for layer in range(layer_count)], 0)
    particle_cache = jnp.concatenate([history_kv, jnp.transpose(new_kv, (0, 2, 1, 3))], axis=2)
    forked_kv = jnp.take(particle_cache, ancestors.astype(jnp.int32), axis=1)
    return (attention_out, forked_kv)
```

```python
import functools
import math
import jax
import jax.numpy as jnp
from jax import lax
from jax.experimental import pallas as pl
from jax.experimental.pallas import tpu as pltpu
from jax.sharding import PartitionSpec as P

HEADS = 64
KV_HEADS = 8
HEAD_DIM = 128
SHARE = HEADS // KV_HEADS
HALF = KV_HEADS * HEAD_DIM
GROUPS = 4
CHUNKS = 2
NEG_FILL = -1e30
MESH = pl.DeviceIdType.MESH
VMEM_LIMIT = 48 * 1024 * 1024


def round_kernel(
    sections,
    shards,
    steps,
    groups,
    hist,
    tok_ref,
    gain_ref,
    pkt_ref,
    prompt_ref,
    okt_ref,
    cache_ref,
    outgoing_ref,
    out_ref,
    incoming_ref,
    slots,
    sent,
    hidden,
    queries,
    pv_ref,
    ov_ref,
    send_sem,
    recv_sem,
    fork_send,
    fork_recv,
    own_sem,
    value_sem,
):
    half = pl.ds(HALF, HALF)
    prompt_values = pltpu.make_async_copy(prompt_ref.at[0, :, half], pv_ref, value_sem.at[0])
    own_values = pltpu.make_async_copy(cache_ref.at[:, :, half], ov_ref, value_sem.at[1])
    prompt_values.start()
    own_values.start()
    sec = lax.axis_index("section")
    me = lax.axis_index("dp")
    after = lax.rem(sec + 1, sections)
    before = lax.rem(sec + sections - 1, sections)
    items = steps * groups
    rows = slots.shape[2]
    width = rows // SHARE
    per = okt_ref.shape[2] // width
    model = HEADS * HEAD_DIM
    chunk_heads = KV_HEADS // CHUNKS

    barrier = pltpu.get_barrier_semaphore()
    pl.semaphore_signal(barrier, inc=1, device_id=(after, me), device_id_type=MESH)
    pl.semaphore_signal(barrier, inc=1, device_id=(before, me), device_id_type=MESH)

    def greet(off, carry):
        peer = lax.rem(me + off, shards)
        pl.semaphore_signal(barrier, inc=1, device_id=(sec, peer), device_id_type=MESH)
        return carry

    lax.fori_loop(1, shards, greet, 0)
    pl.semaphore_wait(barrier, 2 + shards - 1)

    def fork_copy(off):
        peer = lax.rem(me + off, shards)
        return pltpu.make_async_remote_copy(
            src_ref=outgoing_ref.at[peer],
            dst_ref=incoming_ref.at[me],
            send_sem=fork_send.at[off],
            recv_sem=fork_recv.at[off],
            device_id=(sec, peer),
            device_id_type=MESH,
        )

    def fork_start(off, carry):
        fork_copy(off).start()
        return carry

    lax.fori_loop(1, shards, fork_start, 0)
    own = pltpu.make_async_copy(outgoing_ref.at[me], incoming_ref.at[me], own_sem)
    own.start()

    last = sec == sections - 1

    def pass_copy(item, chunk):
        target = jnp.where(last, item + groups, item)
        target = lax.rem(target, items)
        heads = pl.ds(chunk * chunk_heads, chunk_heads)
        return pltpu.make_async_remote_copy(
            src_ref=sent.at[item, heads],
            dst_ref=slots.at[target, heads],
            send_sem=send_sem.at[item, chunk],
            recv_sem=recv_sem.at[target, chunk],
            device_id=(after, me),
            device_id_type=MESH,
        )

    def arrive(item):
        for chunk in range(CHUNKS):
            heads = pl.ds(chunk * chunk_heads, chunk_heads)
            pltpu.make_async_remote_copy(
                src_ref=sent.at[item, heads],
                dst_ref=slots.at[item, heads],
                send_sem=send_sem.at[item, chunk],
                recv_sem=recv_sem.at[item, chunk],
                device_id=(after, me),
                device_id_type=MESH,
            ).wait_recv()

    def inverse_norm(values):
        total = jnp.sum(values * values, axis=0).reshape(width, SHARE, HEAD_DIM)
        total = jnp.sum(jnp.sum(total, axis=2, keepdims=True), axis=1, keepdims=True)
        return lax.rsqrt(total * (1.0 / model) + 1e-05)

    def scaled(values, factor):
        shaped = values.reshape(KV_HEADS, width, SHARE, HEAD_DIM)
        return shaped * factor[None]

    factor = HEAD_DIM ** (-0.5) * math.log2(math.e)
    own_row = lax.broadcasted_iota(jnp.int32, (rows, width * per), 0) // SHARE
    own_col = lax.broadcasted_iota(jnp.int32, (rows, width * per), 1)
    same = own_row == own_col // per
    place = own_col % per

    def step(item, carry):
        now = item // groups
        group = lax.rem(item, groups)

        @pl.when((sec == 0) & (now == 0))
        def _():
            hidden[...] = tok_ref[item].astype(jnp.float32)

        @pl.when((sec == 0) & (now > 0))
        def _():
            arrive(item)
            got = slots[item]
            carried = scaled(got, inverse_norm(got)).reshape(got.shape)
            hidden[...] = tok_ref[item].astype(jnp.float32) + carried

        @pl.when(sec > 0)
        def _():
            arrive(item)
            hidden[...] = slots[item]

        held = hidden[...]
        normed = scaled(held, inverse_norm(held)) * gain_ref[...][:, None]
        queries[...] = normed.reshape(held.shape).astype(jnp.bfloat16)
        present = same & (place <= hist + now)

        for head in range(KV_HEADS):
            lanes = pl.ds(head * HEAD_DIM, HEAD_DIM)
            query = queries[head]
            shared = jnp.dot(query, pkt_ref[lanes, :], preferred_element_type=jnp.float32)
            alone = jnp.dot(
                query, okt_ref[group, lanes, :], preferred_element_type=jnp.float32
            )
            alone = jnp.where(present, alone, NEG_FILL)
            highest = jnp.maximum(
                jnp.max(shared, -1, keepdims=True), jnp.max(alone, -1, keepdims=True)
            )
            shared = jnp.exp2((shared - highest) * factor)
            alone = jnp.exp2((alone - highest) * factor)
            total = jnp.sum(shared, -1, keepdims=True) + jnp.sum(alone, -1, keepdims=True)
            inverse = 1.0 / total
            mixed = jnp.dot(
                (shared * inverse).astype(jnp.bfloat16),
                pv_ref[:, lanes],
                preferred_element_type=jnp.float32,
            )
            mixed = mixed + jnp.dot(
                (alone * inverse).astype(jnp.bfloat16),
                ov_ref[group, :, lanes],
                preferred_element_type=jnp.float32,
            )
            out_ref[item, head] = mixed.astype(jnp.bfloat16)
            sent[item, head] = hidden[head] + mixed
            if head % chunk_heads == chunk_heads - 1:

                @pl.when(jnp.logical_not(last) | (now < steps - 1))
                def _():
                    pass_copy(item, head // chunk_heads).start()

        return carry

    prompt_values.wait()
    own_values.wait()
    lax.fori_loop(0, items, step, 0)

    def sent_done(item, carry):
        @pl.when(jnp.logical_not(last) | (item < items - groups))
        def _():
            for chunk in range(CHUNKS):
                pass_copy(item, chunk).wait_send()

        return carry

    lax.fori_loop(0, items, sent_done, 0)

    def fork_done(off, carry):
        fork_copy(off).wait()
        return carry

    lax.fori_loop(1, shards, fork_done, 0)
    own.wait()


def pick_kernel(count, index_ref, src_ref, dst_ref, sems):
    def begin(i, carry):
        pltpu.make_async_copy(src_ref.at[index_ref[i]], dst_ref.at[i], sems.at[i]).start()
        return carry

    def finish(i, carry):
        pltpu.make_async_copy(src_ref.at[index_ref[i]], dst_ref.at[i], sems.at[i]).wait()
        return carry

    lax.fori_loop(0, count, begin, 0)
    lax.fori_loop(0, count, finish, 0)


def pick(source, index):
    count = index.shape[0]
    return pl.pallas_call(
        functools.partial(pick_kernel, count),
        out_shape=jax.ShapeDtypeStruct((count,) + source.shape[1:], source.dtype),
        in_specs=[
            pl.BlockSpec(memory_space=pltpu.SMEM),
            pl.BlockSpec(memory_space=pl.ANY),
        ],
        out_specs=pl.BlockSpec(memory_space=pl.ANY),
        scratch_shapes=[pltpu.SemaphoreType.DMA((count,))],
    )(index, source)


def local(token_states, norm_gains, prompt_kv, history_kv, new_kv, ancestors):
    sections = lax.axis_size("section")
    shards = lax.axis_size("dp")
    own_index = lax.axis_index("dp")
    part_dev, hist = history_kv.shape[1:3]
    steps = new_kv.shape[1]
    model = token_states.shape[2]
    per = hist + steps
    groups = GROUPS
    width = part_dev // groups
    rows = width * SHARE
    items = steps * groups

    cache = jnp.concatenate([history_kv[0], jnp.transpose(new_kv[0], (1, 0, 2))], axis=1)
    owners = ancestors.reshape(shards, part_dev)
    picked = jnp.max(
        jnp.where(owners // part_dev == own_index, owners % part_dev, 0), axis=1
    )
    outgoing = pick(cache, picked)

    tokens = token_states.reshape(steps, groups, width, KV_HEADS, SHARE, HEAD_DIM)
    tokens = jnp.transpose(tokens, (0, 1, 3, 2, 4, 5)).reshape(items, KV_HEADS, rows, HEAD_DIM)
    gains = norm_gains.reshape(KV_HEADS, SHARE, HEAD_DIM)
    prompt_keys = jnp.transpose(prompt_kv[0, :, :HALF])
    grouped = cache.reshape(groups, width * per, 2 * HALF)
    own_keys = jnp.transpose(grouped[:, :, :HALF], (0, 2, 1))

    whole = pl.BlockSpec(memory_space=pltpu.VMEM)
    prompt_len = prompt_kv.shape[1]
    mixed, incoming = pl.pallas_call(
        functools.partial(round_kernel, sections, shards, steps, groups, hist),
        out_shape=(
            jax.ShapeDtypeStruct((items, KV_HEADS, rows, HEAD_DIM), jnp.bfloat16),
            jax.ShapeDtypeStruct((shards, per, 2 * HALF), jnp.bfloat16),
        ),
        in_specs=[
            whole,
            whole,
            whole,
            pl.BlockSpec(memory_space=pl.ANY),
            whole,
            pl.BlockSpec(memory_space=pl.ANY),
            pl.BlockSpec(memory_space=pl.ANY),
        ],
        out_specs=(whole, pl.BlockSpec(memory_space=pl.ANY)),
        scratch_shapes=[
            pltpu.VMEM((items, KV_HEADS, rows, HEAD_DIM), jnp.float32),
            pltpu.VMEM((items, KV_HEADS, rows, HEAD_DIM), jnp.float32),
            pltpu.VMEM((KV_HEADS, rows, HEAD_DIM), jnp.float32),
            pltpu.VMEM((KV_HEADS, rows, HEAD_DIM), jnp.bfloat16),
            pltpu.VMEM((prompt_len, HALF), jnp.bfloat16),
            pltpu.VMEM((groups, width * per, HALF), jnp.bfloat16),
            pltpu.SemaphoreType.DMA((items, CHUNKS)),
            pltpu.SemaphoreType.DMA((items, CHUNKS)),
            pltpu.SemaphoreType.DMA((shards,)),
            pltpu.SemaphoreType.DMA((shards,)),
            pltpu.SemaphoreType.DMA,
            pltpu.SemaphoreType.DMA((2,)),
        ],
        compiler_params=pltpu.CompilerParams(
            collective_id=0, has_side_effects=True, vmem_limit_bytes=VMEM_LIMIT
        ),
    )(tokens, gains, prompt_keys, prompt_kv, own_keys, grouped, outgoing)

    mixed = mixed.reshape(steps, groups, KV_HEADS, width, SHARE, HEAD_DIM)
    mixed = jnp.transpose(mixed, (0, 1, 3, 2, 4, 5)).reshape(1, steps, part_dev, model)
    own_ancestors = lax.dynamic_slice_in_dim(ancestors, own_index * part_dev, part_dev)
    forked = pick(incoming, own_ancestors // part_dev)
    return (mixed, forked[None])


def solution(mesh):
    in_specs = (
        P(None, "dp", None),
        P("section", None),
        P("section", None, None),
        P("section", "dp", None, None),
        P("section", None, "dp", None),
        P(),
    )
    out_specs = (P("section", None, "dp", None), P("section", "dp", None, None))
    return jax.shard_map(local, mesh=mesh, in_specs=in_specs, out_specs=out_specs, check_vma=False)
```

```python
import functools
import math
import jax
import jax.numpy as jnp
from jax import lax
from jax.experimental import pallas as pl
from jax.experimental.pallas import tpu as pltpu
from jax.sharding import PartitionSpec as P

HEADS = 64
KV_HEADS = 8
HEAD_DIM = 128
SHARE = HEADS // KV_HEADS
HALF = KV_HEADS * HEAD_DIM
GROUPS = 4
CHUNKS = 2
NEG_FILL = -1e30
MESH = pl.DeviceIdType.MESH
VMEM_LIMIT = 56 * 1024 * 1024


def round_kernel(
    sections,
    shards,
    steps,
    groups,
    hist,
    tok_ref,
    gain_ref,
    prompt_ref,
    cache_ref,
    picked_ref,
    source_ref,
    out_ref,
    forked_ref,
    slots,
    sent,
    hidden,
    queries,
    pv_ref,
    ov_ref,
    pkt_ref,
    okt_ref,
    scores,
    weights,
    outgoing,
    incoming,
    send_sem,
    recv_sem,
    fork_send,
    fork_recv,
    value_sem,
):
    prompt_values = pltpu.make_async_copy(prompt_ref.at[0], pv_ref, value_sem.at[0])
    own_values = pltpu.make_async_copy(cache_ref, ov_ref, value_sem.at[1])
    prompt_values.start()
    own_values.start()
    sec = lax.axis_index("section")
    me = lax.axis_index("dp")
    after = lax.rem(sec + 1, sections)
    before = lax.rem(sec + sections - 1, sections)
    items = steps * groups
    rows = slots.shape[2]
    width = rows // SHARE
    per = cache_ref.shape[1]
    model = HEADS * HEAD_DIM
    prompt_len = pv_ref.shape[0]
    part_dev = forked_ref.shape[0]
    chunk_heads = KV_HEADS // CHUNKS

    barrier = pltpu.get_barrier_semaphore()
    pl.semaphore_signal(barrier, inc=1, device_id=(after, me), device_id_type=MESH)
    pl.semaphore_signal(barrier, inc=1, device_id=(before, me), device_id_type=MESH)

    def greet(off, carry):
        peer = lax.rem(me + off, shards)
        pl.semaphore_signal(barrier, inc=1, device_id=(sec, peer), device_id_type=MESH)
        return carry

    lax.fori_loop(1, shards, greet, 0)
    pl.semaphore_wait(barrier, 2 + shards - 1)

    def fork_copy(off):
        peer = lax.rem(me + off, shards)
        return pltpu.make_async_remote_copy(
            src_ref=outgoing.at[off],
            dst_ref=incoming.at[me],
            send_sem=fork_send.at[off],
            recv_sem=fork_recv.at[off],
            device_id=(sec, peer),
            device_id_type=MESH,
        )

    prompt_values.wait()
    own_values.wait()

    def from_cache(index):
        return ov_ref[index]

    def fork_start(off, carry):
        outgoing[off] = from_cache(picked_ref[lax.rem(me + off, shards)])
        fork_copy(off).start()
        return carry

    lax.fori_loop(1, shards, fork_start, 0)
    incoming[me] = from_cache(picked_ref[me])

    last = sec == sections - 1

    def pass_copy(item, chunk):
        target = jnp.where(last, item + groups, item)
        target = lax.rem(target, items)
        heads = pl.ds(chunk * chunk_heads, chunk_heads)
        return pltpu.make_async_remote_copy(
            src_ref=sent.at[item, heads],
            dst_ref=slots.at[target, heads],
            send_sem=send_sem.at[item, chunk],
            recv_sem=recv_sem.at[target, chunk],
            device_id=(after, me),
            device_id_type=MESH,
        )

    def arrive(item):
        for chunk in range(CHUNKS):
            heads = pl.ds(chunk * chunk_heads, chunk_heads)
            pltpu.make_async_remote_copy(
                src_ref=sent.at[item, heads],
                dst_ref=slots.at[item, heads],
                send_sem=send_sem.at[item, chunk],
                recv_sem=recv_sem.at[item, chunk],
                device_id=(after, me),
                device_id_type=MESH,
            ).wait_recv()

    def inverse_norm(values):
        total = jnp.sum(values * values, axis=0).reshape(width, SHARE, HEAD_DIM)
        total = jnp.sum(jnp.sum(total, axis=2, keepdims=True), axis=1, keepdims=True)
        return lax.rsqrt(total * (1.0 / model) + 1e-05)

    def scaled(values, factor):
        shaped = values.reshape(KV_HEADS, width, SHARE, HEAD_DIM)
        return shaped * factor[None]

    factor = HEAD_DIM ** (-0.5) * math.log2(math.e)
    own_row = lax.broadcasted_iota(jnp.int32, (rows, width * per), 0) // SHARE
    own_col = lax.broadcasted_iota(jnp.int32, (rows, width * per), 1)
    same = own_row == own_col // per
    place = own_col % per

    def step(item, carry):
        now = item // groups
        group = lax.rem(item, groups)
        members = pl.ds(group * width, width)

        @pl.when((sec == 0) & (now == 0))
        def _():
            hidden[...] = tok_ref[item].astype(jnp.float32)

        @pl.when((sec == 0) & (now > 0))
        def _():
            arrive(item)
            got = slots[item]
            carried = scaled(got, inverse_norm(got)).reshape(got.shape)
            hidden[...] = tok_ref[item].astype(jnp.float32) + carried

        @pl.when(sec > 0)
        def _():
            arrive(item)
            hidden[...] = slots[item]

        held = hidden[...]
        normed = scaled(held, inverse_norm(held)) * gain_ref[...][:, None]
        queries[...] = normed.reshape(held.shape).astype(jnp.bfloat16)
        present = same & (place <= hist + now)

        for head in range(KV_HEADS):
            lanes = pl.ds(head * HEAD_DIM, HEAD_DIM)
            query = queries[head]
            scores[head, :, :prompt_len] = jnp.dot(
                query, pkt_ref[lanes, :], preferred_element_type=jnp.float32
            )
            alone = jnp.dot(
                query, okt_ref[group, lanes, :], preferred_element_type=jnp.float32
            )
            scores[head, :, prompt_len:] = jnp.where(present, alone, NEG_FILL)

        for head in range(KV_HEADS):
            raw = scores[head]
            highest = jnp.max(raw, -1, keepdims=True)
            raised = jnp.exp2((raw - highest) * factor)
            inverse = 1.0 / jnp.sum(raised, -1, keepdims=True)
            weights[head] = (raised * inverse).astype(jnp.bfloat16)

        for head in range(KV_HEADS):
            lanes = pl.ds(HALF + head * HEAD_DIM, HEAD_DIM)
            mixed = jnp.dot(
                weights[head, :, :prompt_len],
                pv_ref[:, lanes],
                preferred_element_type=jnp.float32,
            )
            mixed = mixed + jnp.dot(
                weights[head, :, prompt_len:],
                ov_ref[members, :, lanes].reshape(width * per, HEAD_DIM),
                preferred_element_type=jnp.float32,
            )
            out_ref[item, head] = mixed.astype(jnp.bfloat16)
            sent[item, head] = hidden[head] + mixed
            if head % chunk_heads == chunk_heads - 1:

                @pl.when(jnp.logical_not(last) | (now < steps - 1))
                def _():
                    pass_copy(item, head // chunk_heads).start()

        return carry

    for head in range(KV_HEADS):
        lanes = pl.ds(head * HEAD_DIM, HEAD_DIM)
        pkt_ref[lanes, :] = pv_ref[:, lanes].T
        for group in range(groups):
            block = ov_ref[pl.ds(group * width, width), :, lanes]
            okt_ref[group, lanes, :] = block.reshape(width * per, HEAD_DIM).T
    lax.fori_loop(0, items, step, 0)

    def sent_done(item, carry):
        @pl.when(jnp.logical_not(last) | (item < items - groups))
        def _():
            for chunk in range(CHUNKS):
                pass_copy(item, chunk).wait_send()

        return carry

    lax.fori_loop(0, items, sent_done, 0)

    def fork_done(off, carry):
        fork_copy(off).wait()
        return carry

    lax.fori_loop(1, shards, fork_done, 0)

    def fork_place(i, carry):
        forked_ref[i] = incoming[source_ref[i]]
        return carry

    lax.fori_loop(0, part_dev, fork_place, 0)


def local(token_states, norm_gains, prompt_kv, history_kv, new_kv, ancestors):
    sections = lax.axis_size("section")
    shards = lax.axis_size("dp")
    own_index = lax.axis_index("dp")
    part_dev, hist = history_kv.shape[1:3]
    steps = new_kv.shape[1]
    model = token_states.shape[2]
    per = hist + steps
    groups = GROUPS
    width = part_dev // groups
    rows = width * SHARE
    items = steps * groups

    cache = jnp.concatenate([history_kv[0], jnp.transpose(new_kv[0], (1, 0, 2))], axis=1)
    owners = ancestors.reshape(shards, part_dev)
    picked = jnp.max(
        jnp.where(owners // part_dev == own_index, owners % part_dev, 0), axis=1
    )
    own_ancestors = lax.dynamic_slice_in_dim(ancestors, own_index * part_dev, part_dev)
    sources = own_ancestors // part_dev

    tokens = token_states.reshape(steps, groups, width, KV_HEADS, SHARE, HEAD_DIM)
    tokens = jnp.transpose(tokens, (0, 1, 3, 2, 4, 5)).reshape(items, KV_HEADS, rows, HEAD_DIM)
    gains = norm_gains.reshape(KV_HEADS, SHARE, HEAD_DIM)

    whole = pl.BlockSpec(memory_space=pltpu.VMEM)
    prompt_len = prompt_kv.shape[1]
    mixed, forked = pl.pallas_call(
        functools.partial(round_kernel, sections, shards, steps, groups, hist),
        out_shape=(
            jax.ShapeDtypeStruct((items, KV_HEADS, rows, HEAD_DIM), jnp.bfloat16),
            jax.ShapeDtypeStruct((part_dev, per, 2 * HALF), jnp.bfloat16),
        ),
        in_specs=[
            whole,
            whole,
            pl.BlockSpec(memory_space=pl.ANY),
            pl.BlockSpec(memory_space=pl.ANY),
            pl.BlockSpec(memory_space=pltpu.SMEM),
            pl.BlockSpec(memory_space=pltpu.SMEM),
        ],
        out_specs=(whole, whole),
        scratch_shapes=[
            pltpu.VMEM((items, KV_HEADS, rows, HEAD_DIM), jnp.float32),
            pltpu.VMEM((items, KV_HEADS, rows, HEAD_DIM), jnp.float32),
            pltpu.VMEM((KV_HEADS, rows, HEAD_DIM), jnp.float32),
            pltpu.VMEM((KV_HEADS, rows, HEAD_DIM), jnp.bfloat16),
            pltpu.VMEM((prompt_len, 2 * HALF), jnp.bfloat16),
            pltpu.VMEM((part_dev, per, 2 * HALF), jnp.bfloat16),
            pltpu.VMEM((HALF, prompt_len), jnp.bfloat16),
            pltpu.VMEM((groups, HALF, width * per), jnp.bfloat16),
            pltpu.VMEM((KV_HEADS, rows, prompt_len + width * per), jnp.float32),
            pltpu.VMEM((KV_HEADS, rows, prompt_len + width * per), jnp.bfloat16),
            pltpu.VMEM((shards, per, 2 * HALF), jnp.bfloat16),
            pltpu.VMEM((shards, per, 2 * HALF), jnp.bfloat16),
            pltpu.SemaphoreType.DMA((items, CHUNKS)),
            pltpu.SemaphoreType.DMA((items, CHUNKS)),
            pltpu.SemaphoreType.DMA((shards,)),
            pltpu.SemaphoreType.DMA((shards,)),
            pltpu.SemaphoreType.DMA((2,)),
        ],
        compiler_params=pltpu.CompilerParams(
            collective_id=0, has_side_effects=True, vmem_limit_bytes=VMEM_LIMIT
        ),
    )(tokens, gains, prompt_kv, cache, picked, sources)

    mixed = mixed.reshape(steps, groups, KV_HEADS, width, SHARE, HEAD_DIM)
    mixed = jnp.transpose(mixed, (0, 1, 3, 2, 4, 5)).reshape(1, steps, part_dev, model)
    return (mixed, forked[None])


def solution(mesh):
    in_specs = (
        P(None, "dp", None),
        P("section", None),
        P("section", None, None),
        P("section", "dp", None, None),
        P("section", None, "dp", None),
        P(),
    )
    out_specs = (P("section", None, "dp", None), P("section", "dp", None, None))
    return jax.shard_map(local, mesh=mesh, in_specs=in_specs, out_specs=out_specs, check_vma=False)
```

```python
import functools
import math
import jax
import jax.numpy as jnp
from jax import lax
from jax.experimental import pallas as pl
from jax.experimental.pallas import tpu as pltpu
from jax.sharding import PartitionSpec as P

HEADS = 64
KV_HEADS = 8
HEAD_DIM = 128
SHARE = HEADS // KV_HEADS
HALF = KV_HEADS * HEAD_DIM
GROUPS = 8
CHUNKS = 2
NEG_FILL = -1e30
MESH = pl.DeviceIdType.MESH
VMEM_LIMIT = 56 * 1024 * 1024


def round_kernel(
    sections,
    shards,
    steps,
    groups,
    hist,
    tok_ref,
    gain_ref,
    prompt_ref,
    cache_ref,
    picked_ref,
    source_ref,
    out_ref,
    forked_ref,
    slots,
    sent,
    hidden,
    queries,
    pv_ref,
    ov_ref,
    pkt_ref,
    okt_ref,
    scores,
    weights,
    mixes,
    outgoing,
    incoming,
    send_sem,
    recv_sem,
    fork_send,
    fork_recv,
    value_sem,
):
    prompt_values = pltpu.make_async_copy(prompt_ref.at[0], pv_ref, value_sem.at[0])
    own_values = pltpu.make_async_copy(cache_ref, ov_ref, value_sem.at[1])
    prompt_values.start()
    own_values.start()
    sec = lax.axis_index("section")
    me = lax.axis_index("dp")
    after = lax.rem(sec + 1, sections)
    before = lax.rem(sec + sections - 1, sections)
    items = steps * groups
    rows = slots.shape[2]
    width = rows // SHARE
    per = cache_ref.shape[1]
    model = HEADS * HEAD_DIM
    prompt_len = pv_ref.shape[0]
    part_dev = forked_ref.shape[0]
    chunk_heads = KV_HEADS // CHUNKS

    barrier = pltpu.get_barrier_semaphore()
    pl.semaphore_signal(barrier, inc=1, device_id=(after, me), device_id_type=MESH)
    pl.semaphore_signal(barrier, inc=1, device_id=(before, me), device_id_type=MESH)

    def greet(off, carry):
        peer = lax.rem(me + off, shards)
        pl.semaphore_signal(barrier, inc=1, device_id=(sec, peer), device_id_type=MESH)
        return carry

    lax.fori_loop(1, shards, greet, 0)
    pl.semaphore_wait(barrier, 2 + shards - 1)

    def fork_copy(off):
        peer = lax.rem(me + off, shards)
        return pltpu.make_async_remote_copy(
            src_ref=outgoing.at[off],
            dst_ref=incoming.at[me],
            send_sem=fork_send.at[off],
            recv_sem=fork_recv.at[off],
            device_id=(sec, peer),
            device_id_type=MESH,
        )

    prompt_values.wait()
    own_values.wait()

    def from_cache(index):
        return ov_ref[index]

    def fork_start(off, carry):
        outgoing[off] = from_cache(picked_ref[lax.rem(me + off, shards)])
        fork_copy(off).start()
        return carry

    lax.fori_loop(1, shards, fork_start, 0)
    incoming[me] = from_cache(picked_ref[me])

    last = sec == sections - 1

    def pass_copy(item, chunk):
        target = jnp.where(last, item + groups, item)
        target = lax.rem(target, items)
        heads = pl.ds(chunk * chunk_heads, chunk_heads)
        return pltpu.make_async_remote_copy(
            src_ref=sent.at[item, heads],
            dst_ref=slots.at[target, heads],
            send_sem=send_sem.at[item, chunk],
            recv_sem=recv_sem.at[target, chunk],
            device_id=(after, me),
            device_id_type=MESH,
        )

    def arrive(item):
        for chunk in range(CHUNKS):
            heads = pl.ds(chunk * chunk_heads, chunk_heads)
            pltpu.make_async_remote_copy(
                src_ref=sent.at[item, heads],
                dst_ref=slots.at[item, heads],
                send_sem=send_sem.at[item, chunk],
                recv_sem=recv_sem.at[item, chunk],
                device_id=(after, me),
                device_id_type=MESH,
            ).wait_recv()

    def inverse_norm(values):
        total = jnp.sum(values * values, axis=0).reshape(width, SHARE, HEAD_DIM)
        total = jnp.sum(jnp.sum(total, axis=2, keepdims=True), axis=1, keepdims=True)
        return lax.rsqrt(total * (1.0 / model) + 1e-05)

    def scaled(values, factor):
        shaped = values.reshape(KV_HEADS, width, SHARE, HEAD_DIM)
        return shaped * factor[None]

    def embedded(item):
        loaded = tok_ref[item].astype(jnp.float32)
        loaded = loaded.reshape(width, KV_HEADS, SHARE, HEAD_DIM)
        parts = [loaded[:, head].reshape(rows, HEAD_DIM) for head in range(KV_HEADS)]
        return jnp.stack(parts, axis=0)

    factor = HEAD_DIM ** (-0.5) * math.log2(math.e)
    own_row = lax.broadcasted_iota(jnp.int32, (rows, width * per), 0) // SHARE
    own_col = lax.broadcasted_iota(jnp.int32, (rows, width * per), 1)
    same = own_row == own_col // per
    place = own_col % per

    def step(item, carry):
        now = item // groups
        group = lax.rem(item, groups)
        members = pl.ds(group * width, width)

        @pl.when((sec == 0) & (now == 0))
        def _():
            hidden[...] = embedded(item)

        @pl.when((sec == 0) & (now > 0))
        def _():
            arrive(item)
            got = slots[item]
            carried = scaled(got, inverse_norm(got)).reshape(got.shape)
            hidden[...] = embedded(item) + carried

        @pl.when(sec > 0)
        def _():
            arrive(item)
            hidden[...] = slots[item]

        held = hidden[...]
        normed = scaled(held, inverse_norm(held)) * gain_ref[...][:, None]
        queries[...] = normed.reshape(held.shape).astype(jnp.bfloat16)
        present = same & (place <= hist + now)

        for head in range(KV_HEADS):
            lanes = pl.ds(head * HEAD_DIM, HEAD_DIM)
            query = queries[head]
            scores[head, :, :prompt_len] = jnp.dot(
                query, pkt_ref[lanes, :], preferred_element_type=jnp.float32
            )
            alone = jnp.dot(
                query, okt_ref[group, lanes, :], preferred_element_type=jnp.float32
            )
            scores[head, :, prompt_len:] = jnp.where(present, alone, NEG_FILL)

        for head in range(KV_HEADS):
            raw = scores[head]
            highest = jnp.max(raw, -1, keepdims=True)
            raised = jnp.exp2((raw - highest) * factor)
            inverse = 1.0 / jnp.sum(raised, -1, keepdims=True)
            weights[head] = (raised * inverse).astype(jnp.bfloat16)

        for head in range(KV_HEADS):
            lanes = pl.ds(HALF + head * HEAD_DIM, HEAD_DIM)
            mixed = jnp.dot(
                weights[head, :, :prompt_len],
                pv_ref[:, lanes],
                preferred_element_type=jnp.float32,
            )
            mixed = mixed + jnp.dot(
                weights[head, :, prompt_len:],
                ov_ref[members, :, lanes].reshape(width * per, HEAD_DIM),
                preferred_element_type=jnp.float32,
            )
            mixes[:, pl.ds(head * SHARE, SHARE), :] = mixed.reshape(width, SHARE, HEAD_DIM)
            sent[item, head] = hidden[head] + mixed
            if head % chunk_heads == chunk_heads - 1:

                @pl.when(jnp.logical_not(last) | (now < steps - 1))
                def _():
                    pass_copy(item, head // chunk_heads).start()

        out_ref[item] = mixes[...].astype(jnp.bfloat16)
        return carry

    for head in range(KV_HEADS):
        lanes = pl.ds(head * HEAD_DIM, HEAD_DIM)
        pkt_ref[lanes, :] = pv_ref[:, lanes].T
        for group in range(groups):
            block = ov_ref[pl.ds(group * width, width), :, lanes]
            okt_ref[group, lanes, :] = block.reshape(width * per, HEAD_DIM).T
    lax.fori_loop(0, items, step, 0)

    def sent_done(item, carry):
        @pl.when(jnp.logical_not(last) | (item < items - groups))
        def _():
            for chunk in range(CHUNKS):
                pass_copy(item, chunk).wait_send()

        return carry

    lax.fori_loop(0, items, sent_done, 0)

    def fork_done(off, carry):
        fork_copy(off).wait()
        return carry

    lax.fori_loop(1, shards, fork_done, 0)

    def fork_place(i, carry):
        forked_ref[i] = incoming[source_ref[i]]
        return carry

    lax.fori_loop(0, part_dev, fork_place, 0)


def local(token_states, norm_gains, prompt_kv, history_kv, new_kv, ancestors):
    sections = lax.axis_size("section")
    shards = lax.axis_size("dp")
    own_index = lax.axis_index("dp")
    part_dev, hist = history_kv.shape[1:3]
    steps = new_kv.shape[1]
    model = token_states.shape[2]
    per = hist + steps
    groups = GROUPS
    width = part_dev // groups
    rows = width * SHARE
    items = steps * groups

    cache = jnp.concatenate([history_kv[0], jnp.transpose(new_kv[0], (1, 0, 2))], axis=1)
    owners = ancestors.reshape(shards, part_dev)
    picked = jnp.max(
        jnp.where(owners // part_dev == own_index, owners % part_dev, 0), axis=1
    )
    own_ancestors = lax.dynamic_slice_in_dim(ancestors, own_index * part_dev, part_dev)
    sources = own_ancestors // part_dev

    tokens = token_states.reshape(items, width, HEADS, HEAD_DIM)
    gains = norm_gains.reshape(KV_HEADS, SHARE, HEAD_DIM)

    whole = pl.BlockSpec(memory_space=pltpu.VMEM)
    prompt_len = prompt_kv.shape[1]
    mixed, forked = pl.pallas_call(
        functools.partial(round_kernel, sections, shards, steps, groups, hist),
        out_shape=(
            jax.ShapeDtypeStruct((items, width, HEADS, HEAD_DIM), jnp.bfloat16),
            jax.ShapeDtypeStruct((part_dev, per, 2 * HALF), jnp.bfloat16),
        ),
        in_specs=[
            whole,
            whole,
            pl.BlockSpec(memory_space=pl.ANY),
            pl.BlockSpec(memory_space=pl.ANY),
            pl.BlockSpec(memory_space=pltpu.SMEM),
            pl.BlockSpec(memory_space=pltpu.SMEM),
        ],
        out_specs=(whole, whole),
        scratch_shapes=[
            pltpu.VMEM((items, KV_HEADS, rows, HEAD_DIM), jnp.float32),
            pltpu.VMEM((items, KV_HEADS, rows, HEAD_DIM), jnp.float32),
            pltpu.VMEM((KV_HEADS, rows, HEAD_DIM), jnp.float32),
            pltpu.VMEM((KV_HEADS, rows, HEAD_DIM), jnp.bfloat16),
            pltpu.VMEM((prompt_len, 2 * HALF), jnp.bfloat16),
            pltpu.VMEM((part_dev, per, 2 * HALF), jnp.bfloat16),
            pltpu.VMEM((HALF, prompt_len), jnp.bfloat16),
            pltpu.VMEM((groups, HALF, width * per), jnp.bfloat16),
            pltpu.VMEM((KV_HEADS, rows, prompt_len + width * per), jnp.float32),
            pltpu.VMEM((KV_HEADS, rows, prompt_len + width * per), jnp.bfloat16),
            pltpu.VMEM((width, HEADS, HEAD_DIM), jnp.float32),
            pltpu.VMEM((shards, per, 2 * HALF), jnp.bfloat16),
            pltpu.VMEM((shards, per, 2 * HALF), jnp.bfloat16),
            pltpu.SemaphoreType.DMA((items, CHUNKS)),
            pltpu.SemaphoreType.DMA((items, CHUNKS)),
            pltpu.SemaphoreType.DMA((shards,)),
            pltpu.SemaphoreType.DMA((shards,)),
            pltpu.SemaphoreType.DMA((2,)),
        ],
        compiler_params=pltpu.CompilerParams(
            collective_id=0, has_side_effects=True, vmem_limit_bytes=VMEM_LIMIT
        ),
    )(tokens, gains, prompt_kv, cache, picked, sources)

    mixed = mixed.reshape(1, steps, part_dev, model)
    return (mixed, forked[None])


def solution(mesh):
    in_specs = (
        P(None, "dp", None),
        P("section", None),
        P("section", None, None),
        P("section", "dp", None, None),
        P("section", None, "dp", None),
        P(),
    )
    out_specs = (P("section", None, "dp", None), P("section", "dp", None, None))
    return jax.shard_map(local, mesh=mesh, in_specs=in_specs, out_specs=out_specs, check_vma=False)
```
